512 devices in a mesh: req: 32 (over z, core), seq: 16 (over y, x).
Axes of the slice: x: 4, y: 4, z: 16, core: 2. Of those that a mesh axis runs over, the one named last changes fastest.
Arguments:
- queries: bfloat16 [2, 32, 8192], P(None, 'req'), may hold values from -150 to 150
- kv_cache: bfloat16 [32, 12288, 2048], P('req', 'seq'), may hold values from -6 to 6
- context_length: int32 [32], P('req'), may hold values from 1 to 12288, as said below
- block_count: int32 [32], P('req'), may hold values from 1 to 128, as said below
- anchor_codes: int32 [32, 128, 2048], P(None, 'req', 'seq'), may hold values from -64 to 63
- delta_codes: int32 [32, 128, 16, 2048], P(None, 'req', None, 'seq'), may hold values from -64 to 63
- block_scale: float32 [32, 128, 2048], P(None, 'req', 'seq'), may hold values from 0.008 to 0.03
Outputs:
- attended: bfloat16 [2, 32, 8192], P(None, 'req', 'seq')
The draws below stay inside these ranges and needn't reach their ends.
Inputs may be any that keep to these rules, and one draw needn't show every extreme that they name: Some request has context_length 12288. Some request has block_count 128.
All inputs are finite; a program needn't handle non-finite values.
Results may differ from the reference program's by a relative error of at most 0.0075.
Values may be sent and summed in bfloat16 or wider, within the bound.
A program may use at most 64 MiB of HBM per device.

```python
import math
import jax
import jax.numpy as jnp
from jax import lax

H = 64
KVH = 8
HD = 128
BLK = 16
STEPS = 2
REQS = 32
CTX = 12288
NBLK = 128
CHAN = 2048


def draw_queries(key, part):
    key = jax.random.fold_in(key, 11)
    key_base = jax.random.fold_in(key, 0)
    base = jax.random.truncated_normal(key_base, -6.0, 6.0, (STEPS, REQS, H * HD), jnp.float32)
    return (2.75 * base).astype(jnp.bfloat16)


def draw_context_length(key, part):
    key = jax.random.fold_in(key, 5)
    key_lengths, key_chosen = jax.random.split(key)
    lengths = jax.random.randint(key_lengths, (REQS,), 1, CTX + 1)
    chosen = jax.random.randint(key_chosen, (), 0, REQS)
    return jnp.where(jnp.arange(REQS) == chosen, CTX, lengths).astype(jnp.int32)


def draw_block_count(key, part):
    key = jax.random.fold_in(key, 7)
    key_counts, key_chosen = jax.random.split(key)
    counts = jax.random.randint(key_counts, (REQS,), 1, NBLK + 1)
    chosen = jax.random.randint(key_chosen, (), 0, REQS)
    return jnp.where(jnp.arange(REQS) == chosen, NBLK, counts).astype(jnp.int32)


def touch_ends(values, stream_key, low, largest):
    longest = values.shape.index(max(values.shape))
    spots = []
    for shift in (0, 1):
        where = [jax.random.randint(jax.random.fold_in(stream_key, axis), (), 0, length) for axis, length in enumerate(values.shape)]
        where[longest] = (where[longest] + shift) % values.shape[longest]
        spots.append(tuple(where))
    return values.at[spots[0]].set(low).at[spots[1]].set(largest)


def steps_of(stream_key, extent, shards, smallest, largest):
    factor_of, own = 1.0, jax.random.fold_in(stream_key, 6)
    for dim, parts in shards:
        draws = jnp.exp(jax.random.uniform(jax.random.fold_in(own, dim), (parts,), jnp.float32, smallest / len(shards), largest / len(shards)))
        factor_of = factor_of * jnp.repeat(draws, extent[dim] // parts).reshape([-1 if axis == dim else 1 for axis in range(len(extent))])
    return factor_of


def noise(key, extent, width, most, cuts=(), kind=jnp.bfloat16):
    values = width * jax.random.normal(key, extent, jnp.float32)
    if cuts:
        values = values * steps_of(key, extent, cuts, -0.22, 0.18)
    return jnp.clip(values, -most, most).astype(kind)


def setup_inputs(seed: int = 0) -> dict:
    key_of = jax.random.split(jax.random.key(seed), 8)
    queries = draw_queries(jax.random.fold_in(key_of[7], 71), 0)
    kv_cache = noise(key_of[1], (REQS, CTX, CHAN), 1.0, 6.0, ((0, 32), (1, 16)))
    context_length = draw_context_length(jax.random.fold_in(key_of[7], 71), 0)
    block_count = draw_block_count(jax.random.fold_in(key_of[7], 71), 0)
    anchor_codes = touch_ends(jax.random.randint(key_of[4], (REQS, NBLK, CHAN), -64, 64), jax.random.fold_in(key_of[4], 1), -64, 63).astype(jnp.int32)
    delta_codes = touch_ends(jax.random.randint(key_of[5], (REQS, NBLK, BLK, CHAN), -64, 64), jax.random.fold_in(key_of[5], 1), -64, 63).astype(jnp.int32)
    block_scale = jnp.clip(jnp.exp(math.log(0.03) - 1.3217558 * jax.random.uniform(key_of[6], (REQS, NBLK, CHAN), jnp.float32) ** steps_of(key_of[6], (REQS, NBLK, CHAN), ((1, 32), (2, 16)), -0.2, 0.2)), 0.008, 0.03)
    return {"queries": queries, "kv_cache": kv_cache, "context_length": context_length, "block_count": block_count, "anchor_codes": anchor_codes, "delta_codes": delta_codes, "block_scale": block_scale}


def attend_one(query_rows, rows, live):
    row_count = rows.shape[0]
    groups = H // KVH
    heads = query_rows.astype(jnp.float32).reshape(STEPS, KVH, groups, HD)
    keys = rows[:, :KVH * HD].astype(jnp.float32).reshape(row_count, KVH, HD)
    values = rows[:, KVH * HD:].astype(jnp.float32).reshape(row_count, KVH, HD)
    scores = jnp.einsum("skgd,nkd->skgn", heads, keys) * (HD ** -0.5)
    scores = jnp.where(live, scores, jnp.float32(-1e30))
    highest = jnp.max(scores, axis=-1, keepdims=True)
    weights = jnp.where(live, jnp.exp(scores - highest), jnp.float32(0.0))
    totals = jnp.sum(weights, axis=-1)
    rounded = lax.optimization_barrier(weights.astype(jnp.bfloat16)).astype(jnp.float32)
    summed = jnp.einsum("skgn,nkd->skgd", rounded, values)
    return (summed / totals[..., None]).reshape(STEPS, H * HD).astype(jnp.bfloat16)


def one_request(inputs):
    query_rows, cache_rows, length, blocks, anchors, deltas, scales = inputs
    arrived = (scales[:, None, :] * (anchors[:, None, :] + deltas).astype(jnp.float32)).astype(jnp.bfloat16)
    rows = jnp.concatenate([cache_rows, arrived.reshape(NBLK * BLK, CHAN)], axis=0)
    cached_live = jnp.arange(CTX, dtype=jnp.int32) < length
    block_live = jnp.repeat(jnp.arange(NBLK, dtype=jnp.int32) < blocks, BLK)
    live = jnp.concatenate([cached_live, block_live], axis=0)
    return attend_one(query_rows, rows, live)


def reference(queries, kv_cache, context_length, block_count, anchor_codes, delta_codes, block_scale):
    results = lax.map(one_request, (jnp.swapaxes(queries, 0, 1), kv_cache, context_length, block_count, anchor_codes, delta_codes, block_scale))
    return jnp.swapaxes(results, 0, 1)
```

```python
import jax
import jax.numpy as jnp
from jax import lax
from jax.experimental import pallas as pl
from jax.experimental.pallas import tpu as pltpu
from jax.sharding import PartitionSpec as P

H = 64
KVH = 8
HD = 128
GROUP = H // KVH
STEPS = 2
ROWS = GROUP * STEPS
MESH = pl.DeviceIdType.MESH
F32 = jnp.float32
BF16 = jnp.bfloat16
NEG = -1e30


def packed(summed, highest, totals):
    lane = lax.broadcasted_iota(jnp.int32, (8, HD), 1)
    coarse = totals.astype(BF16).astype(F32)
    stats = jnp.where(lane < 32, highest, jnp.where(lane < 64, coarse, totals - coarse))
    return jnp.concatenate([summed, stats], axis=0).astype(BF16)


def partial_attention(query, keys, values, live):
    scores = lax.dot_general(
        query, keys, (((1,), (1,)), ((), ())), preferred_element_type=F32
    ) * HD ** (-0.5)
    scores = jnp.where(live, scores, NEG)
    highest = jnp.max(scores, axis=1, keepdims=True).astype(BF16).astype(F32)
    weights = jnp.where(live, jnp.exp(scores - highest), 0.0)
    totals = jnp.sum(weights, axis=1, keepdims=True)
    summed = jnp.dot(weights.astype(BF16), values, preferred_element_type=F32)
    return highest, totals, summed


def kernel(
    q_hbm, cache_hbm, length_hbm, count_hbm, anchor_hbm, delta_hbm, scale_hbm,
    out_ref,
    q_v, cache_v, length_s, count_s, anchor_v, delta_v, scale_v,
    decoded, kv, q_all, count_mine, count_all, cached_msg, arrived_msg, inbox,
    load_sem, own_sem, q_send, q_recv, c_send, c_recv, kv_send, kv_recv,
    part_send, late_send, in_recv,
):
    r, s = lax.axis_index("req"), lax.axis_index("seq")
    z, c = r // 2, lax.rem(r, 2)
    h, k = s // 8, lax.rem(s, 8)
    slots = cache_hbm.shape[0]

    def place(zz, cc, ss):
        return (2 * zz + cc, ss)

    kin = [(1, 0), (0, 1), (1, 1)]

    def kin_place(dc, dh):
        return place(z, lax.rem(c + dc, 2), lax.rem(s + 8 * dh, 16))

    barrier = pltpu.get_barrier_semaphore()
    for d in range(1, 16):
        pl.semaphore_signal(barrier, inc=1, device_id=place(lax.rem(z + d, 16), c, s), device_id_type=MESH)
        pl.semaphore_signal(barrier, inc=1, device_id=place(z, c, lax.rem(s + d, 16)), device_id_type=MESH)
    for dc, dh in ((1, 0), (1, 1)):
        pl.semaphore_signal(barrier, inc=1, device_id=kin_place(dc, dh), device_id_type=MESH)

    loads = [
        pltpu.make_async_copy(src, dst, load_sem.at[n])
        for n, (src, dst) in enumerate(
            (
                (q_hbm, q_v),
                (count_hbm, count_s),
                (anchor_hbm, anchor_v),
                (scale_hbm, scale_v),
                (delta_hbm, delta_v),
                (length_hbm, length_s),
                (cache_hbm, cache_v),
            )
        )
    ]
    for load in loads:
        load.start()
    for load in loads[:5]:
        load.wait()
    count_mine[...] = jnp.full(count_mine.shape, count_s[0], jnp.int32)

    def decode(i, carry):
        for hh in range(2):
            for cc in range(2):
                q = 4 * i + 2 * hh + cc
                for b in range(4):
                    codes = anchor_v[q, b : b + 1, :] + delta_v[q, b]
                    decoded[hh, cc, i, 16 * b : 16 * b + 16, :] = (
                        scale_v[q, b : b + 1, :] * codes.astype(F32)
                    ).astype(BF16)
        return carry

    lax.fori_loop(0, 8, decode, 0)

    pl.semaphore_wait(barrier, 32)

    asks = lax.rem(z, 2) == h
    my_query = q_v.at[pl.ds(pl.multiple_of(ROWS * k, ROWS), ROWS), :]
    sent = []
    for d in (8, 7, 9, 6, 10, 5, 11, 4, 12, 3, 13, 2, 14, 1, 15):
        to = place(lax.rem(z + d, 16), c, s)
        for src, dst, ssem, rsem in (
            (my_query, q_all.at[z // 2], q_send.at[d - 1], q_recv),
            (count_mine.at[0], count_all.at[z // 2], c_send.at[d - 1], c_recv),
        ):
            sent.append(
                pltpu.make_async_remote_copy(
                    src_ref=src, dst_ref=dst, send_sem=ssem, recv_sem=rsem, device_id=to, device_id_type=MESH
                )
            )

    @pl.when(asks)
    def _():
        for copy in sent:
            copy.start()
        pltpu.make_async_copy(my_query, q_all.at[z // 2], q_recv).start()
        pltpu.make_async_copy(count_mine.at[0], count_all.at[z // 2], c_recv).start()

    def landing(hh, cc):
        return kv.at[hh, :, pl.ds(pl.multiple_of(64 * cc, 64), 64), :]

    swaps = []
    for n, (dc, dh) in enumerate(kin):
        swaps.append(
            pltpu.make_async_remote_copy(
                src_ref=decoded.at[lax.rem(h + dh, 2), lax.rem(c + dc, 2)],
                dst_ref=landing(h, c),
                send_sem=kv_send.at[n],
                recv_sem=kv_recv.at[n],
                device_id=kin_place(dc, dh),
                device_id_type=MESH,
            )
        )
        swaps[-1].start()
    own = pltpu.make_async_copy(decoded.at[h, c], landing(h, c), own_sem)
    own.start()

    for load in loads[5:]:
        load.wait()
    cached_live = s * slots + lax.broadcasted_iota(jnp.int32, (1, slots), 1) < length_s[0]
    for head in range(KVH):
        highest, totals, summed = partial_attention(
            q_v[ROWS * head : ROWS * head + ROWS, :],
            cache_v[:, HD * head : HD * head + HD],
            cache_v[:, HD * (KVH + head) : HD * (KVH + head) + HD],
            cached_live,
        )
        for e in range(2):
            part = slice(8 * e, 8 * e + 8)
            cached_msg[2 * head + e] = packed(summed[part], highest[part], totals[part])
    spread = []
    for d in range(1, 16):
        to = lax.rem(s + d, 16)
        spread.append(
            pltpu.make_async_remote_copy(
                src_ref=cached_msg.at[to],
                dst_ref=inbox.at[s],
                send_sem=part_send.at[d - 1],
                recv_sem=in_recv,
                device_id=place(z, c, to),
                device_id_type=MESH,
            )
        )
        spread[-1].start()
    pltpu.make_async_copy(cached_msg.at[s], inbox.at[s], in_recv).start()

    pltpu.make_async_copy(q_all, q_all, q_recv).wait()
    pltpu.make_async_copy(count_all, count_all, c_recv).wait()
    own.wait()
    for swap in swaps:
        swap.wait_recv()
    block = 8 * z + lax.broadcasted_iota(jnp.int32, (1, HD), 1) // 16
    for i in range(8):
        highest, totals, summed = partial_attention(
            q_all[i], kv[0, i], kv[1, i], block < count_all[i]
        )
        for e in range(2):
            part = slice(8 * e, 8 * e + 8)
            arrived_msg[2 * i + e] = packed(summed[part], highest[part], totals[part])
    returns = []
    for i in range(8):
        for e in range(2):
            zz, ss = 2 * i + h, 2 * k + e
            here = jnp.logical_and(zz == z, ss == s)
            copy = pltpu.make_async_remote_copy(
                src_ref=arrived_msg.at[2 * i + e],
                dst_ref=inbox.at[16 + z],
                send_sem=late_send.at[2 * i + e],
                recv_sem=in_recv,
                device_id=place(zz, c, ss),
                device_id_type=MESH,
            )
            returns.append((here, copy))

            @pl.when(jnp.logical_not(here))
            def _():
                copy.start()

            @pl.when(here)
            def _():
                pltpu.make_async_copy(arrived_msg.at[2 * i + e], inbox.at[16 + z], in_recv).start()

    pltpu.make_async_copy(inbox, inbox, in_recv).wait()
    parts = inbox[...].astype(F32)
    stats = parts[:, 8:, :]
    shrink = jnp.exp(stats - jnp.max(stats, axis=0, keepdims=True))[:, :, 0:1]
    totals = jnp.sum(shrink * (stats[:, :, 32:33] + stats[:, :, 64:65]), axis=0)
    summed = jnp.sum(shrink * parts[:, :8, :], axis=0)
    out_ref[...] = (summed / totals).astype(BF16)

    @pl.when(asks)
    def _():
        for copy in sent:
            copy.wait_send()

    for copy in swaps + spread:
        copy.wait_send()
    for here, copy in returns:

        @pl.when(jnp.logical_not(here))
        def _():
            copy.wait_send()


def shards(queries, kv_cache, context_length, block_count, anchor_codes, delta_codes, block_scale):
    slots = kv_cache.shape[1]
    rows = queries.reshape(STEPS, H, HD).swapaxes(0, 1).reshape(STEPS * H, HD)
    out = pl.pallas_call(
        kernel,
        out_shape=jax.ShapeDtypeStruct((8, HD), BF16),
        in_specs=[pl.BlockSpec(memory_space=pltpu.HBM)] * 7,
        out_specs=pl.BlockSpec(memory_space=pltpu.VMEM),
        scratch_shapes=[
            pltpu.VMEM((STEPS * H, HD), BF16),
            pltpu.VMEM((slots, 2 * KVH * HD), BF16),
            pltpu.SMEM((1,), jnp.int32),
            pltpu.SMEM((1,), jnp.int32),
            pltpu.VMEM((32, 4, HD), jnp.int32),
            pltpu.VMEM((32, 4, 16, HD), jnp.int32),
            pltpu.VMEM((32, 4, HD), F32),
            pltpu.VMEM((2, 2, 8, 64, HD), BF16),
            pltpu.VMEM((2, 8, 128, HD), BF16),
            pltpu.VMEM((8, ROWS, HD), BF16),
            pltpu.VMEM((1, 1, HD), jnp.int32),
            pltpu.VMEM((8, 1, HD), jnp.int32),
            pltpu.VMEM((16, 16, HD), BF16),
            pltpu.VMEM((16, 16, HD), BF16),
            pltpu.VMEM((32, 16, HD), BF16),
            pltpu.SemaphoreType.DMA((7,)),
            pltpu.SemaphoreType.DMA,
            pltpu.SemaphoreType.DMA((15,)),
            pltpu.SemaphoreType.DMA,
            pltpu.SemaphoreType.DMA((15,)),
            pltpu.SemaphoreType.DMA,
            pltpu.SemaphoreType.DMA((3,)),
            pltpu.SemaphoreType.DMA((3,)),
            pltpu.SemaphoreType.DMA((15,)),
            pltpu.SemaphoreType.DMA((16,)),
            pltpu.SemaphoreType.DMA,
        ],
        compiler_params=pltpu.CompilerParams(
            collective_id=0, has_side_effects=True, vmem_limit_bytes=60 << 20
        ),
    )(rows, kv_cache[0], context_length, block_count, anchor_codes, delta_codes, block_scale)
    return out.reshape(4, STEPS, HD).swapaxes(0, 1).reshape(STEPS, 1, 4 * HD)


def solution(mesh):
    placed = (
        P(None, "req", None),
        P("req", "seq", None),
        P("req"),
        P("req"),
        P(None, "req", "seq"),
        P(None, "req", None, "seq"),
        P(None, "req", "seq"),
    )
    return jax.shard_map(
        shards, mesh=mesh, in_specs=placed, out_specs=P(None, "req", "seq"), check_vma=False
    )
```

```python
import jax
import jax.numpy as jnp
from jax import lax
from jax.experimental import pallas as pl
from jax.experimental.pallas import tpu as pltpu
from jax.sharding import PartitionSpec as P

H = 64
KVH = 8
HD = 128
GROUP = H // KVH
STEPS = 2
ROWS = GROUP * STEPS
MESH = pl.DeviceIdType.MESH
F32 = jnp.float32
BF16 = jnp.bfloat16
NEG = -1e30
UP = (4, 3, 2, 1)
DOWN = (6, 5, 4, 3, 2, 1)
ONWARD = (5, 4, 3, 2, 1)
PARTS = 4


def packed(summed, highest, totals):
    lane = lax.broadcasted_iota(jnp.int32, (8, HD), 1)
    coarse = totals.astype(BF16).astype(F32)
    stats = jnp.where(lane < 32, highest, jnp.where(lane < 64, coarse, totals - coarse))
    return jnp.concatenate([summed, stats], axis=0).astype(BF16)


def partial_attention(query, keys, values, live):
    scores = lax.dot_general(
        query, keys, (((1,), (1,)), ((), ())), preferred_element_type=F32
    ) * HD ** (-0.5)
    scores = jnp.where(live, scores, NEG)
    highest = jnp.max(scores, axis=1, keepdims=True).astype(BF16).astype(F32)
    weights = jnp.where(live, jnp.exp(scores - highest), 0.0)
    totals = jnp.sum(weights, axis=1, keepdims=True)
    summed = jnp.dot(weights.astype(BF16), values, preferred_element_type=F32)
    return highest, totals, summed


def kernel(
    q_hbm, cache_hbm, length_s, count_s, anchor_hbm, delta_hbm, scale_hbm,
    out_ref,
    q_v, cache_v, anchor_v, delta_v, scale_v,
    decoded, kv, q_all, count_mine, count_all, cached_msg, arrived_msg, inbox,
    load_sem, q_send, q_recv, c_send, c_recv, kv_send, kv_recv,
    part_send, late_send, in_recv,
):
    r, s = lax.axis_index("req"), lax.axis_index("seq")
    z, c = r // 2, lax.rem(r, 2)
    side, head = s // 8, lax.rem(s, 8)
    h, k = lax.rem(s, 2), s // 2
    slots = cache_hbm.shape[0]

    def place(zz, cc, ss):
        return (2 * zz + cc, ss)

    barrier = pltpu.get_barrier_semaphore()
    asks = lax.rem(z, 2) == h
    over = s + 1 - 2 * h

    def along(d):
        return lax.rem(z + d + 16, 16)

    def greet(zz, ss):
        pl.semaphore_signal(barrier, inc=1, device_id=place(zz, c, ss), device_id_type=MESH)

    for d in range(1, 16):
        greet(z, lax.rem(s + d, 16))

    for sd in range(2):
        pl.semaphore_signal(barrier, inc=1, device_id=place(z, 1 - c, k + 8 * sd), device_id_type=MESH)

    @pl.when(asks)
    def _():
        for d in (2, 4):
            greet(along(-d), s)
        for d in (2, 4, 6):
            greet(along(d), over)

    @pl.when(jnp.logical_not(asks))
    def _():
        for d in (1, 3, 5):
            greet(along(-d), s)
            greet(along(d), over)

    loads = [
        pltpu.make_async_copy(src, dst, load_sem.at[n])
        for n, (src, dst) in enumerate(
            (
                (q_hbm, q_v),
                (anchor_hbm, anchor_v),
                (scale_hbm, scale_v),
                (delta_hbm, delta_v),
                (cache_hbm, cache_v),
            )
        )
    ]
    for load in loads:
        load.start()
    for load in loads[:4]:
        load.wait()
    count_mine[...] = jnp.full(count_mine.shape, count_s[0], jnp.int32)

    def decode(i, carry):
        for hh in range(2):
            for cc in range(2):
                q = 4 * i + 2 * hh + cc
                for b in range(4):
                    codes = anchor_v[q, b : b + 1, :] + delta_v[q, b]
                    decoded[hh, cc, i, 16 * b : 16 * b + 16, :] = (
                        scale_v[q, b : b + 1, :] * codes.astype(F32)
                    ).astype(BF16)
        return carry

    lax.fori_loop(0, 8, decode, 0)

    def cached_rows():
        for load in loads[4:]:
            load.wait()
        live = s * slots + lax.broadcasted_iota(jnp.int32, (1, slots), 1) < length_s[0]
        for head in range(KVH):
            highest, totals, summed = partial_attention(
                q_v[ROWS * head : ROWS * head + ROWS, :],
                cache_v[:, HD * head : HD * head + HD],
                cache_v[:, HD * (KVH + head) : HD * (KVH + head) + HD],
                live,
            )
            for e in range(2):
                part = slice(8 * e, 8 * e + 8)
                cached_msg[2 * head + e] = packed(summed[part], highest[part], totals[part])

    @pl.when(z < 8)
    def _():
        cached_rows()

    pl.semaphore_wait(barrier, jnp.where(asks, 22, 23))

    my_query = q_v.at[pl.ds(pl.multiple_of(ROWS * k, ROWS), ROWS), :]

    def bring(query, count, queries, counts, n, to):
        return [
            pltpu.make_async_remote_copy(
                src_ref=src, dst_ref=dst, send_sem=ssem.at[n], recv_sem=rsem.at[n], device_id=to, device_id_type=MESH
            )
            for src, dst, ssem, rsem in (
                (query, queries, q_send, q_recv),
                (count, counts, c_send, c_recv),
            )
        ]

    def slot_of(zz):
        return q_all.at[zz // 2], count_all.at[zz // 2]

    def came(queries, counts, n):
        for ref, sem in ((queries, q_recv), (counts, c_recv)):
            pltpu.make_async_copy(ref, ref, sem.at[n]).wait()

    mine = (my_query, count_mine.at[0])
    up, down, onward = [], [], []
    for d in UP:
        up += bring(*mine, *slot_of(z), d, place(along(d), c, s))
    for d in DOWN:
        down += bring(*mine, *slot_of(z), 16 - d, place(along(-d), c, over))
    for d in ONWARD:
        onward += bring(*slot_of(along(-4)), *slot_of(along(-4)), 4 + d, place(along(d), c, s))

    @pl.when(asks)
    def _():
        for copy in up:
            copy.start()
        for src, dst, sem in zip(mine, slot_of(z), (q_recv, c_recv)):
            pltpu.make_async_copy(src, dst, sem.at[0]).start()

    @pl.when(jnp.logical_not(asks))
    def _():
        for copy in down:
            copy.start()

    def landing(sd, cc, part):
        rows = pl.ds(pl.multiple_of(64 * cc, 64), 64)
        return kv.at[sd, 2 * part : 2 * part + 2, rows, :]

    swaps = []
    for part in range(PARTS):
        for hh in range(2):
            for cc in range(2):
                src = decoded.at[hh, cc, 2 * part : 2 * part + 2]
                here = jnp.logical_and(s == 2 * head + hh, c == cc)
                arrives = kv_recv.at[side, c, part]
                copy = pltpu.make_async_remote_copy(
                    src_ref=src,
                    dst_ref=landing(side, c, part),
                    send_sem=kv_send.at[4 * part + 2 * hh + cc],
                    recv_sem=arrives,
                    device_id=place(z, cc, 2 * head + hh),
                    device_id_type=MESH,
                )
                swaps.append((here, copy))

                @pl.when(jnp.logical_not(here))
                def _():
                    copy.start()

                @pl.when(here)
                def _():
                    pltpu.make_async_copy(src, landing(side, c, part), arrives).start()

    @pl.when(z >= 8)
    def _():
        cached_rows()

    @pl.when(asks)
    def _():
        came(*slot_of(along(-4)), 4)
        for copy in onward:
            copy.start()

    spread = []
    for d in range(1, 16):
        to = lax.rem(s + d, 16)
        spread.append(
            pltpu.make_async_remote_copy(
                src_ref=cached_msg.at[to],
                dst_ref=inbox.at[s],
                send_sem=part_send.at[d - 1],
                recv_sem=in_recv,
                device_id=place(z, c, to),
                device_id_type=MESH,
            )
        )
        spread[-1].start()
    pltpu.make_async_copy(cached_msg.at[s], inbox.at[s], in_recv).start()

    block = 8 * z + lax.broadcasted_iota(jnp.int32, (1, HD), 1) // 16
    returns = []
    for i in range(8):
        if i % 2 == 0:
            for sd in range(2):
                for cc in range(2):
                    ref = landing(sd, cc, i // 2)
                    pltpu.make_async_copy(ref, ref, kv_recv.at[sd, cc, i // 2]).wait()
        zz = 2 * i + h
        d = along(-zz)

        @pl.when(d != 4)
        def _():
            came(q_all.at[i], count_all.at[i], d)

        highest, totals, summed = partial_attention(
            q_all[i], kv[0, i], kv[1, i], block < count_all[i]
        )
        for e in range(2):
            part = slice(8 * e, 8 * e + 8)
            arrived_msg[2 * i + e] = packed(summed[part], highest[part], totals[part])
            ss = 2 * k + e
            here = jnp.logical_and(zz == z, ss == s)
            copy = pltpu.make_async_remote_copy(
                src_ref=arrived_msg.at[2 * i + e],
                dst_ref=inbox.at[16 + z],
                send_sem=late_send.at[2 * i + e],
                recv_sem=in_recv,
                device_id=place(zz, c, ss),
                device_id_type=MESH,
            )
            returns.append((here, copy))

            @pl.when(jnp.logical_not(here))
            def _():
                copy.start()

            @pl.when(here)
            def _():
                pltpu.make_async_copy(arrived_msg.at[2 * i + e], inbox.at[16 + z], in_recv).start()

    pltpu.make_async_copy(inbox, inbox, in_recv).wait()
    parts = inbox[...].astype(F32)
    stats = parts[:, 8:, :]
    shrink = jnp.exp(stats - jnp.max(stats, axis=0, keepdims=True))[:, :, 0:1]
    totals = jnp.sum(shrink * (stats[:, :, 32:33] + stats[:, :, 64:65]), axis=0)
    summed = jnp.sum(shrink * parts[:, :8, :], axis=0)
    out_ref[...] = (summed / totals).astype(BF16)

    @pl.when(asks)
    def _():
        for copy in up + onward:
            copy.wait_send()

    @pl.when(jnp.logical_not(asks))
    def _():
        for copy in down:
            copy.wait_send()

    for copy in spread:
        copy.wait_send()
    for here, copy in swaps + returns:

        @pl.when(jnp.logical_not(here))
        def _():
            copy.wait_send()


def shards(queries, kv_cache, context_length, block_count, anchor_codes, delta_codes, block_scale):
    slots = kv_cache.shape[1]
    rows = queries.reshape(STEPS, H, HD).swapaxes(0, 1).reshape(STEPS * H, HD)
    out = pl.pallas_call(
        kernel,
        out_shape=jax.ShapeDtypeStruct((8, HD), BF16),
        in_specs=[pl.BlockSpec(memory_space=pltpu.HBM)] * 2
        + [pl.BlockSpec(memory_space=pltpu.SMEM)] * 2
        + [pl.BlockSpec(memory_space=pltpu.HBM)] * 3,
        out_specs=pl.BlockSpec(memory_space=pltpu.VMEM),
        scratch_shapes=[
            pltpu.VMEM((STEPS * H, HD), BF16),
            pltpu.VMEM((slots, 2 * KVH * HD), BF16),
            pltpu.VMEM((32, 4, HD), jnp.int32),
            pltpu.VMEM((32, 4, 16, HD), jnp.int32),
            pltpu.VMEM((32, 4, HD), F32),
            pltpu.VMEM((2, 2, 8, 64, HD), BF16),
            pltpu.VMEM((2, 8, 128, HD), BF16),
            pltpu.VMEM((8, ROWS, HD), BF16),
            pltpu.VMEM((1, 1, HD), jnp.int32),
            pltpu.VMEM((8, 1, HD), jnp.int32),
            pltpu.VMEM((16, 16, HD), BF16),
            pltpu.VMEM((16, 16, HD), BF16),
            pltpu.VMEM((32, 16, HD), BF16),
            pltpu.SemaphoreType.DMA((5,)),
            pltpu.SemaphoreType.DMA((16,)),
            pltpu.SemaphoreType.DMA((16,)),
            pltpu.SemaphoreType.DMA((16,)),
            pltpu.SemaphoreType.DMA((16,)),
            pltpu.SemaphoreType.DMA((16,)),
            pltpu.SemaphoreType.DMA((2, 2, PARTS)),
            pltpu.SemaphoreType.DMA((15,)),
            pltpu.SemaphoreType.DMA((16,)),
            pltpu.SemaphoreType.DMA,
        ],
        compiler_params=pltpu.CompilerParams(
            collective_id=0, has_side_effects=True, vmem_limit_bytes=56541184
        ),
    )(rows, kv_cache[0], context_length, block_count, anchor_codes, delta_codes, block_scale)
    return out.reshape(4, STEPS, HD).swapaxes(0, 1).reshape(STEPS, 1, 4 * HD)


def solution(mesh):
    placed = (
        P(None, "req", None),
        P("req", "seq", None),
        P("req"),
        P("req"),
        P(None, "req", "seq"),
        P(None, "req", None, "seq"),
        P(None, "req", "seq"),
    )
    return jax.shard_map(
        shards, mesh=mesh, in_specs=placed, out_specs=P(None, "req", "seq"), check_vma=False
    )
```

```python
import functools

import jax
import jax.numpy as jnp
from jax import lax
from jax.experimental import pallas as pl
from jax.experimental.pallas import tpu as pltpu
from jax.sharding import PartitionSpec as P

H = 64
KVH = 8
HD = 128
GROUP = H // KVH
STEPS = 2
ROWS = GROUP * STEPS
MESH = pl.DeviceIdType.MESH
F32 = jnp.float32
BF16 = jnp.bfloat16
NEG = -1e30
UP = (4, 3, 2, 1)
DOWN = (7, 6, 5, 4, 3, 2, 1)
ONWARD = (6, 5, 4, 3, 2, 1)


def goes_down(z, d):
    return z >= {7: 12, 6: 4}.get(d, 0)


def goes_on(z, d):
    if d == 6:
        return jnp.logical_and(z >= 4, z < 8)
    return z >= {5: 4}.get(d, 0)


PARTS = ((0, 2), (2, 4), (4, 8))


def packed(summed, highest, totals):
    lane = lax.broadcasted_iota(jnp.int32, (8, HD), 1)
    coarse = totals.astype(BF16).astype(F32)
    stats = jnp.where(lane < 32, highest, jnp.where(lane < 64, coarse, totals - coarse))
    return jnp.concatenate([summed, stats], axis=0).astype(BF16)


def partial_attention(query, keys, values, live):
    scores = lax.dot_general(
        query, keys, (((1,), (1,)), ((), ())), preferred_element_type=F32
    ) * HD ** (-0.5)
    scores = jnp.where(live, scores, NEG)
    highest = jnp.max(scores, axis=1, keepdims=True).astype(BF16).astype(F32)
    weights = jnp.where(live, jnp.exp(scores - highest), 0.0)
    totals = jnp.sum(weights, axis=1, keepdims=True)
    summed = jnp.dot(weights.astype(BF16), values, preferred_element_type=F32)
    return highest, totals, summed


def kernel(
    q_hbm, cache_hbm, length_s, count_s, anchor_hbm, delta_hbm, scale_hbm,
    out_ref,
    q_v, cache_v, anchor_v, delta_v, scale_v,
    decoded, kv, q_all, mine, cached_msg, arrived_msg, inbox,
    load_sem, q_send, q_recv, kv_send, kv_recv,
    part_send, late_send, in_recv,
):
    r, s = lax.axis_index("req"), lax.axis_index("seq")
    z, c = r // 2, lax.rem(r, 2)
    side, head = s // 8, lax.rem(s, 8)
    h, k = lax.rem(s, 2), s // 2
    slots = cache_hbm.shape[0]

    def place(zz, cc, ss):
        return (2 * zz + cc, ss)

    barrier = pltpu.get_barrier_semaphore()
    asks = lax.rem(z, 2) == h
    over = s + 1 - 2 * h

    def along(d):
        return lax.rem(z + d + 16, 16)

    def greet(zz, ss):
        pl.semaphore_signal(barrier, inc=1, device_id=place(zz, c, ss), device_id_type=MESH)

    def greet_senders(ups, downs):
        for d in ups:
            pl.when(goes_on(along(-d), d))(functools.partial(greet, along(-d), s))
        for d in downs:
            pl.when(goes_down(along(d), d))(functools.partial(greet, along(d), over))

    pl.when(asks)(functools.partial(greet_senders, (6, 4, 2), (6, 4, 2)))
    pl.when(jnp.logical_not(asks))(functools.partial(greet_senders, (5, 3, 1), (7, 5, 3, 1)))
    n_on = sum(goes_on(z, d).astype(jnp.int32) for d in ONWARD)
    n_down = sum(goes_down(z, d).astype(jnp.int32) for d in DOWN)
    greeted_by = 17 + jnp.where(asks, n_on, n_down)

    for sd in range(2):
        pl.semaphore_signal(barrier, inc=1, device_id=place(z, 1 - c, k + 8 * sd), device_id_type=MESH)
    for d in range(1, 16):
        greet(z, lax.rem(s + d, 16))

    loads = [
        pltpu.make_async_copy(src, dst, load_sem.at[n])
        for n, (src, dst) in enumerate(
            (
                (q_hbm, q_v),
                (anchor_hbm, anchor_v),
                (scale_hbm, scale_v),
                (delta_hbm, delta_v),
                (cache_hbm, cache_v),
            )
        )
    ]
    for load in loads:
        load.start()
    for load in loads[:4]:
        load.wait()
    mine[:ROWS] = q_v[pl.ds(pl.multiple_of(ROWS * k, ROWS), ROWS), :]
    mine[ROWS:] = jnp.full((16, HD), count_s[0], jnp.int32).astype(F32).astype(BF16)

    def decode(i, carry):
        for hh in range(2):
            for cc in range(2):
                q = 4 * i + 2 * hh + cc
                for b in range(4):
                    codes = anchor_v[q, b : b + 1, :] + delta_v[q, b]
                    decoded[hh, cc, i, 16 * b : 16 * b + 16, :] = (
                        scale_v[q, b : b + 1, :] * codes.astype(F32)
                    ).astype(BF16)
        return carry

    lax.fori_loop(0, 8, decode, 0)

    def cached_rows():
        for load in loads[4:]:
            load.wait()
        live = s * slots + lax.broadcasted_iota(jnp.int32, (1, slots), 1) < length_s[0]
        for head in range(KVH):
            highest, totals, summed = partial_attention(
                q_v[ROWS * head : ROWS * head + ROWS, :],
                cache_v[:, HD * head : HD * head + HD],
                cache_v[:, HD * (KVH + head) : HD * (KVH + head) + HD],
                live,
            )
            for e in range(2):
                part = slice(8 * e, 8 * e + 8)
                cached_msg[2 * head + e] = packed(summed[part], highest[part], totals[part])

    early = jnp.logical_and(z < 8, jnp.logical_or(r > 0, s > 0))

    @pl.when(early)
    def _():
        cached_rows()

    pl.semaphore_wait(barrier, greeted_by)

    def bring(asked, zz, to):
        return pltpu.make_async_remote_copy(
            src_ref=asked,
            dst_ref=q_all.at[zz // 2],
            send_sem=q_send,
            recv_sem=q_recv.at[zz // 2],
            device_id=to,
            device_id_type=MESH,
        )

    def came(i):
        pltpu.make_async_copy(q_all.at[i], q_all.at[i], q_recv.at[i]).wait()

    below = along(-4)
    up = [(d > 0, bring(mine, z, place(along(d), c, s))) for d in UP]
    down = [(goes_down(z, d), bring(mine, z, place(along(-d), c, over))) for d in DOWN]
    onward = [(goes_on(z, d), bring(q_all.at[below // 2], below, place(along(d), c, s))) for d in ONWARD]

    def each(conditional, act):
        for wanted, copy in conditional:
            pl.when(wanted)(functools.partial(act, copy))

    def start(copy):
        copy.start()

    @pl.when(asks)
    def _():
        each(up, start)
        pltpu.make_async_copy(mine, q_all.at[z // 2], q_recv.at[z // 2]).start()

    @pl.when(jnp.logical_not(asks))
    def _():
        each(down, start)

    def landing(sd, cc, part):
        first, last = PARTS[part]
        return kv.at[sd, first:last, pl.ds(pl.multiple_of(64 * cc, 64), 64), :]

    def swap(part):
        first, last = PARTS[part]
        for hh in range(2):
            for cc in range(2):
                src = decoded.at[hh, cc, first:last]
                here = jnp.logical_and(s == 2 * head + hh, c == cc)
                arrives = kv_recv.at[part]
                copy = pltpu.make_async_remote_copy(
                    src_ref=src,
                    dst_ref=landing(side, c, part),
                    send_sem=kv_send,
                    recv_sem=arrives,
                    device_id=place(z, cc, 2 * head + hh),
                    device_id_type=MESH,
                )

                @pl.when(jnp.logical_not(here))
                def _():
                    copy.start()

                @pl.when(here)
                def _():
                    pltpu.make_async_copy(src, landing(side, c, part), arrives).start()

    def pass_on():
        came(below // 2)
        each(onward, start)

    middle = jnp.logical_and(z >= 4, z < 8)
    swap(0)
    pl.when(jnp.logical_and(asks, middle))(pass_on)
    swap(1)
    swap(2)

    @pl.when(jnp.logical_not(early))
    def _():
        cached_rows()


    spread = []
    for d in range(1, 16):
        to = lax.rem(s + d, 16)
        spread.append(
            pltpu.make_async_remote_copy(
                src_ref=cached_msg.at[to],
                dst_ref=inbox.at[s],
                send_sem=part_send,
                recv_sem=in_recv.at[0],
                device_id=place(z, c, to),
                device_id_type=MESH,
            )
        )

    def send_cached():
        for copy in spread:
            copy.start()
        pltpu.make_async_copy(cached_msg.at[s], inbox.at[s], in_recv.at[0]).start()

    pl.when(early)(send_cached)
    block = (8 * z + lax.broadcasted_iota(jnp.int32, (1, HD), 1) // 16).astype(F32)
    for i in range(8):
        if i == 0:
            pl.when(jnp.logical_and(asks, jnp.logical_not(middle)))(pass_on)
        if i == 2:
            pl.when(jnp.logical_not(early))(send_cached)
        for part in range(len(PARTS)):
            if i == PARTS[part][0]:
                ref = kv.at[:, slice(*PARTS[part])]
                pltpu.make_async_copy(ref, ref, kv_recv.at[part]).wait()
        zz = 2 * i + h
        d = along(-zz)

        @pl.when(d != 4)
        def _():
            came(i)

        highest, totals, summed = partial_attention(
            q_all[i, :ROWS], kv[0, i], kv[1, i], block < q_all[i, ROWS : ROWS + 1].astype(F32)
        )
        for e in range(2):
            part = slice(8 * e, 8 * e + 8)
            arrived_msg[2 * i + e] = packed(summed[part], highest[part], totals[part])
            ss = 2 * k + e
            here = jnp.logical_and(zz == z, ss == s)
            copy = pltpu.make_async_remote_copy(
                src_ref=arrived_msg.at[2 * i + e],
                dst_ref=inbox.at[16 + z],
                send_sem=late_send,
                recv_sem=in_recv.at[1],
                device_id=place(zz, c, ss),
                device_id_type=MESH,
            )

            @pl.when(jnp.logical_not(here))
            def _():
                copy.start()

            @pl.when(here)
            def _():
                pltpu.make_async_copy(arrived_msg.at[2 * i + e], inbox.at[16 + z], in_recv.at[1]).start()

    def merged(first, last):
        parts = inbox[first:last].astype(F32)
        stats = parts[:, 8:, :]
        highest = jnp.max(stats, axis=0)
        shrink = jnp.exp(stats - highest)[:, :, 0:1]
        totals = jnp.sum(shrink * (stats[:, :, 32:33] + stats[:, :, 64:65]), axis=0)
        return highest[:, 0:1], totals, jnp.sum(shrink * parts[:, :8, :], axis=0)

    def wait_inbox(first, last, n):
        pltpu.make_async_copy(inbox.at[first:last], inbox.at[first:last], in_recv.at[n]).wait()

    wait_inbox(0, 16, 0)
    cached_highest, cached_totals, cached_summed = merged(0, 16)

    def left(ref, sem):
        pltpu.make_async_copy(ref, ref, sem).wait()

    for n in range(len(ONWARD) + 1):
        pl.when(jnp.logical_and(asks, n_on == n))(
            functools.partial(left, inbox.at[: 2 * (n + len(UP))], q_send)
        )
    for n in range(1, len(DOWN) + 1):
        pl.when(jnp.logical_and(jnp.logical_not(asks), n_down == n))(
            functools.partial(left, inbox.at[: 2 * n], q_send)
        )
    kept = jnp.logical_or(s == 0, s == 15)
    pl.when(kept)(functools.partial(left, delta_v.at[:12], kv_send))
    pl.when(jnp.logical_not(kept))(functools.partial(left, delta_v.at[:16], kv_send))
    left(inbox.at[:15], part_send)
    pl.when(asks)(functools.partial(left, inbox.at[:15], late_send))
    pl.when(jnp.logical_not(asks))(functools.partial(left, inbox.at[:16], late_send))

    wait_inbox(16, 32, 1)
    highest, totals, summed = merged(16, 32)
    top = jnp.maximum(highest, cached_highest)
    shrink, cached_shrink = jnp.exp(highest - top), jnp.exp(cached_highest - top)
    out_ref[...] = (
        (summed * shrink + cached_summed * cached_shrink)
        / (totals * shrink + cached_totals * cached_shrink)
    ).astype(BF16)


def shards(queries, kv_cache, context_length, block_count, anchor_codes, delta_codes, block_scale):
    slots = kv_cache.shape[1]
    rows = queries.reshape(STEPS, H, HD).swapaxes(0, 1).reshape(STEPS * H, HD)
    out = pl.pallas_call(
        kernel,
        out_shape=jax.ShapeDtypeStruct((8, HD), BF16),
        in_specs=[pl.BlockSpec(memory_space=pltpu.HBM)] * 2
        + [pl.BlockSpec(memory_space=pltpu.SMEM)] * 2
        + [pl.BlockSpec(memory_space=pltpu.HBM)] * 3,
        out_specs=pl.BlockSpec(memory_space=pltpu.VMEM),
        scratch_shapes=[
            pltpu.VMEM((STEPS * H, HD), BF16),
            pltpu.VMEM((slots, 2 * KVH * HD), BF16),
            pltpu.VMEM((32, 4, HD), jnp.int32),
            pltpu.VMEM((32, 4, 16, HD), jnp.int32),
            pltpu.VMEM((32, 4, HD), F32),
            pltpu.VMEM((2, 2, 8, 64, HD), BF16),
            pltpu.VMEM((2, 8, 128, HD), BF16),
            pltpu.VMEM((8, ROWS + 16, HD), BF16),
            pltpu.VMEM((ROWS + 16, HD), BF16),
            pltpu.VMEM((16, 16, HD), BF16),
            pltpu.VMEM((16, 16, HD), BF16),
            pltpu.VMEM((32, 16, HD), BF16),
            pltpu.SemaphoreType.DMA((5,)),
            pltpu.SemaphoreType.DMA,
            pltpu.SemaphoreType.DMA((8,)),
            pltpu.SemaphoreType.DMA,
            pltpu.SemaphoreType.DMA((len(PARTS),)),
            pltpu.SemaphoreType.DMA,
            pltpu.SemaphoreType.DMA,
            pltpu.SemaphoreType.DMA((2,)),
        ],
        compiler_params=pltpu.CompilerParams(
            collective_id=0, has_side_effects=True, vmem_limit_bytes=56541184
        ),
    )(rows, kv_cache[0], context_length, block_count, anchor_codes, delta_codes, block_scale)
    return out.reshape(4, STEPS, HD).swapaxes(0, 1).reshape(STEPS, 1, 4 * HD)


def solution(mesh):
    placed = (
        P(None, "req", None),
        P("req", "seq", None),
        P("req"),
        P("req"),
        P(None, "req", "seq"),
        P(None, "req", None, "seq"),
        P(None, "req", "seq"),
    )
    return jax.shard_map(
        shards, mesh=mesh, in_specs=placed, out_specs=P(None, "req", "seq"), check_vma=False
    )
```

```python
import functools

import jax
import jax.numpy as jnp
from jax import lax
from jax.experimental import pallas as pl
from jax.experimental.pallas import tpu as pltpu
from jax.sharding import PartitionSpec as P

H = 64
KVH = 8
HD = 128
GROUP = H // KVH
STEPS = 2
ROWS = GROUP * STEPS
MESH = pl.DeviceIdType.MESH
F32 = jnp.float32
BF16 = jnp.bfloat16
NEG = -1e30
UP = (4, 3, 2, 1)
DOWN = (7, 6, 5, 4, 3, 2, 1)
ONWARD = (6, 5, 4, 3, 2, 1)


def goes_down(z, d):
    return z >= {7: 12, 6: 4}.get(d, 0)


def goes_on(z, d):
    if d == 6:
        return jnp.logical_and(z >= 4, z < 8)
    return z >= {5: 4}.get(d, 0)


PARTS = ((0, 2), (2, 4), (4, 8))


def packed(summed, highest, totals):
    lane = lax.broadcasted_iota(jnp.int32, (8, HD), 1)
    coarse = totals.astype(BF16).astype(F32)
    stats = jnp.where(lane < 32, highest, jnp.where(lane < 64, coarse, totals - coarse))
    return jnp.concatenate([summed, stats], axis=0).astype(BF16)


def partial_attention(query, keys, values, live):
    scores = lax.dot_general(
        query, keys, (((1,), (1,)), ((), ())), preferred_element_type=F32
    ) * HD ** (-0.5)
    scores = jnp.where(live, scores, NEG)
    highest = jnp.max(scores, axis=1, keepdims=True).astype(BF16).astype(F32)
    weights = jnp.where(live, jnp.exp(scores - highest), 0.0)
    totals = jnp.sum(weights, axis=1, keepdims=True)
    summed = jnp.dot(weights.astype(BF16), values, preferred_element_type=F32)
    return highest, totals, summed


def kernel(
    q_hbm, cache_hbm, length_s, count_s, anchor_hbm, delta_hbm, scale_hbm,
    out_ref,
    q_v, cache_v, anchor_v, delta_v, scale_v,
    decoded, kv, q_all, mine, cached_msg, arrived_msg, inbox,
    load_sem, q_send, q_recv, kv_send, kv_recv,
    part_send, late_send, in_recv,
):
    r, s = lax.axis_index("req"), lax.axis_index("seq")
    z, c = r // 2, lax.rem(r, 2)
    side, head = s // 8, lax.rem(s, 8)
    h, k = lax.rem(s, 2), s // 2
    slots = cache_hbm.shape[0]

    def place(zz, cc, ss):
        return (2 * zz + cc, ss)

    barrier = pltpu.get_barrier_semaphore()
    asks = lax.rem(z, 2) == h
    over = s + 1 - 2 * h

    def along(d):
        return lax.rem(z + d + 16, 16)

    def greet(zz, ss):
        pl.semaphore_signal(barrier, inc=1, device_id=place(zz, c, ss), device_id_type=MESH)

    def greet_senders(ups, downs):
        for d in ups:
            pl.when(goes_on(along(-d), d))(functools.partial(greet, along(-d), s))
        for d in downs:
            pl.when(goes_down(along(d), d))(functools.partial(greet, along(d), over))

    pl.when(asks)(functools.partial(greet_senders, (6, 4, 2), (6, 4, 2)))
    pl.when(jnp.logical_not(asks))(functools.partial(greet_senders, (5, 3, 1), (7, 5, 3, 1)))
    n_on = sum(goes_on(z, d).astype(jnp.int32) for d in ONWARD)
    n_down = sum(goes_down(z, d).astype(jnp.int32) for d in DOWN)
    greeted_by = 17 + jnp.where(asks, n_on, n_down)

    for sd in range(2):
        pl.semaphore_signal(barrier, inc=1, device_id=place(z, 1 - c, k + 8 * sd), device_id_type=MESH)
    for d in range(1, 16):
        greet(z, lax.rem(s + d, 16))

    loads = [
        pltpu.make_async_copy(src, dst, load_sem.at[n])
        for n, (src, dst) in enumerate(
            (
                (q_hbm, q_v),
                (anchor_hbm, anchor_v),
                (scale_hbm, scale_v),
                (delta_hbm, delta_v),
                (cache_hbm, cache_v),
            )
        )
    ]
    for load in loads:
        load.start()
    for load in loads[:4]:
        load.wait()
    mine[:ROWS] = q_v[pl.ds(pl.multiple_of(ROWS * k, ROWS), ROWS), :]
    mine[ROWS:] = jnp.full((16, HD), count_s[0], jnp.int32).astype(F32).astype(BF16)

    def decode(i, carry):
        for hh in range(2):
            for cc in range(2):
                q = 4 * i + 2 * hh + cc
                for b in range(4):
                    codes = anchor_v[q, b : b + 1, :] + delta_v[q, b]
                    decoded[hh, cc, i, 16 * b : 16 * b + 16, :] = (
                        scale_v[q, b : b + 1, :] * codes.astype(F32)
                    ).astype(BF16)
        return carry

    lax.fori_loop(0, 8, decode, 0)

    def cached_rows():
        for load in loads[4:]:
            load.wait()
        live = s * slots + lax.broadcasted_iota(jnp.int32, (1, slots), 1) < length_s[0]
        for head in range(KVH):
            highest, totals, summed = partial_attention(
                q_v[ROWS * head : ROWS * head + ROWS, :],
                cache_v[:, HD * head : HD * head + HD],
                cache_v[:, HD * (KVH + head) : HD * (KVH + head) + HD],
                live,
            )
            for e in range(2):
                part = slice(8 * e, 8 * e + 8)
                cached_msg[2 * head + e] = packed(summed[part], highest[part], totals[part])

    early = jnp.logical_and(z < 8, jnp.logical_or(r > 0, s > 0))

    @pl.when(early)
    def _():
        cached_rows()

    pl.semaphore_wait(barrier, greeted_by)

    def bring(asked, zz, to):
        return pltpu.make_async_remote_copy(
            src_ref=asked,
            dst_ref=q_all.at[zz // 2],
            send_sem=q_send,
            recv_sem=q_recv.at[zz // 2],
            device_id=to,
            device_id_type=MESH,
        )

    def came(i):
        pltpu.make_async_copy(q_all.at[i], q_all.at[i], q_recv.at[i]).wait()

    below = along(-4)
    up = [(d > 0, bring(mine, z, place(along(d), c, s))) for d in UP]
    down = [(goes_down(z, d), bring(mine, z, place(along(-d), c, over))) for d in DOWN]
    onward = [(goes_on(z, d), bring(q_all.at[below // 2], below, place(along(d), c, s))) for d in ONWARD]

    def each(conditional, act):
        for wanted, copy in conditional:
            pl.when(wanted)(functools.partial(act, copy))

    def start(copy):
        copy.start()

    @pl.when(asks)
    def _():
        each(up, start)
        pltpu.make_async_copy(mine, q_all.at[z // 2], q_recv.at[z // 2]).start()

    @pl.when(jnp.logical_not(asks))
    def _():
        each(down, start)

    def landing(sd, cc, part):
        first, last = PARTS[part]
        return kv.at[sd, first:last, pl.ds(pl.multiple_of(64 * cc, 64), 64), :]

    def swap(part):
        first, last = PARTS[part]
        for hh in range(2):
            for cc in range(2):
                src = decoded.at[hh, cc, first:last]
                here = jnp.logical_and(s == 2 * head + hh, c == cc)
                arrives = kv_recv.at[part]
                copy = pltpu.make_async_remote_copy(
                    src_ref=src,
                    dst_ref=landing(side, c, part),
                    send_sem=kv_send,
                    recv_sem=arrives,
                    device_id=place(z, cc, 2 * head + hh),
                    device_id_type=MESH,
                )

                @pl.when(jnp.logical_not(here))
                def _():
                    copy.start()

                @pl.when(here)
                def _():
                    pltpu.make_async_copy(src, landing(side, c, part), arrives).start()

    def pass_on():
        came(below // 2)
        each(onward, start)

    middle = jnp.logical_and(z >= 4, z < 8)
    swap(0)
    pl.when(jnp.logical_and(asks, middle))(pass_on)
    swap(1)
    swap(2)

    @pl.when(jnp.logical_not(early))
    def _():
        cached_rows()


    spread = []
    for d in range(1, 16):
        to = lax.rem(s + d, 16)
        spread.append(
            pltpu.make_async_remote_copy(
                src_ref=cached_msg.at[to],
                dst_ref=inbox.at[s],
                send_sem=part_send,
                recv_sem=in_recv.at[0],
                device_id=place(z, c, to),
                device_id_type=MESH,
            )
        )

    def send_cached():
        for copy in spread:
            copy.start()
        pltpu.make_async_copy(cached_msg.at[s], inbox.at[s], in_recv.at[0]).start()

    pl.when(early)(send_cached)
    block = (8 * z + lax.broadcasted_iota(jnp.int32, (1, HD), 1) // 16).astype(F32)
    for i in range(8):
        if i == 0:
            pl.when(jnp.logical_and(asks, jnp.logical_not(middle)))(pass_on)
        if i == 2:
            pl.when(jnp.logical_not(early))(send_cached)
        for part in range(len(PARTS)):
            if i == PARTS[part][0]:
                ref = kv.at[:, slice(*PARTS[part])]
                pltpu.make_async_copy(ref, ref, kv_recv.at[part]).wait()
        zz = 2 * i + h
        d = along(-zz)

        @pl.when(d != 4)
        def _():
            came(i)

        highest, totals, summed = partial_attention(
            q_all[i, :ROWS], kv[0, i], kv[1, i], block < q_all[i, ROWS:].astype(F32)
        )
        for e in range(2):
            part = slice(8 * e, 8 * e + 8)
            arrived_msg[2 * i + e] = packed(summed[part], highest[part], totals[part])
            ss = 2 * k + e
            here = jnp.logical_and(zz == z, ss == s)
            copy = pltpu.make_async_remote_copy(
                src_ref=arrived_msg.at[2 * i + e],
                dst_ref=inbox.at[16 + z],
                send_sem=late_send,
                recv_sem=in_recv.at[1],
                device_id=place(zz, c, ss),
                device_id_type=MESH,
            )

            @pl.when(jnp.logical_not(here))
            def _():
                copy.start()

            @pl.when(here)
            def _():
                pltpu.make_async_copy(arrived_msg.at[2 * i + e], inbox.at[16 + z], in_recv.at[1]).start()

    def merged(first, last):
        parts = inbox[first:last].astype(F32)
        stats = parts[:, 8:, :]
        highest = jnp.max(stats, axis=0)
        shrink = jnp.exp(stats - highest)[:, :, 0:1]
        totals = jnp.sum(shrink * (stats[:, :, 32:33] + stats[:, :, 64:65]), axis=0)
        return highest[:, 0:1], totals, jnp.sum(shrink * parts[:, :8, :], axis=0)

    def wait_inbox(first, last, n):
        pltpu.make_async_copy(inbox.at[first:last], inbox.at[first:last], in_recv.at[n]).wait()

    wait_inbox(0, 16, 0)
    cached_highest, cached_totals, cached_summed = merged(0, 16)

    def left(ref, sem):
        pltpu.make_async_copy(ref, ref, sem).wait()

    for n in range(len(ONWARD) + 1):
        pl.when(jnp.logical_and(asks, n_on == n))(
            functools.partial(left, inbox.at[: 2 * (n + len(UP))], q_send)
        )
    for n in range(1, len(DOWN) + 1):
        pl.when(jnp.logical_and(jnp.logical_not(asks), n_down == n))(
            functools.partial(left, inbox.at[: 2 * n], q_send)
        )
    kept = jnp.logical_or(s == 0, s == 15)
    pl.when(kept)(functools.partial(left, delta_v.at[:12], kv_send))
    pl.when(jnp.logical_not(kept))(functools.partial(left, delta_v.at[:16], kv_send))
    left(inbox.at[:15], part_send)
    pl.when(asks)(functools.partial(left, inbox.at[:15], late_send))
    pl.when(jnp.logical_not(asks))(functools.partial(left, inbox.at[:16], late_send))

    wait_inbox(16, 32, 1)
    highest, totals, summed = merged(16, 32)
    top = jnp.maximum(highest, cached_highest)
    shrink, cached_shrink = jnp.exp(highest - top), jnp.exp(cached_highest - top)
    out_ref[...] = (
        (summed * shrink + cached_summed * cached_shrink)
        / (totals * shrink + cached_totals * cached_shrink)
    ).astype(BF16)


def shards(queries, kv_cache, context_length, block_count, anchor_codes, delta_codes, block_scale):
    slots = kv_cache.shape[1]
    rows = queries.reshape(STEPS, H, HD).swapaxes(0, 1).reshape(STEPS * H, HD)
    out = pl.pallas_call(
        kernel,
        out_shape=jax.ShapeDtypeStruct((8, HD), BF16),
        in_specs=[pl.BlockSpec(memory_space=pltpu.HBM)] * 2
        + [pl.BlockSpec(memory_space=pltpu.SMEM)] * 2
        + [pl.BlockSpec(memory_space=pltpu.HBM)] * 3,
        out_specs=pl.BlockSpec(memory_space=pltpu.VMEM),
        scratch_shapes=[
            pltpu.VMEM((STEPS * H, HD), BF16),
            pltpu.VMEM((slots, 2 * KVH * HD), BF16),
            pltpu.VMEM((32, 4, HD), jnp.int32),
            pltpu.VMEM((32, 4, 16, HD), jnp.int32),
            pltpu.VMEM((32, 4, HD), F32),
            pltpu.VMEM((2, 2, 8, 64, HD), BF16),
            pltpu.VMEM((2, 8, 128, HD), BF16),
            pltpu.VMEM((8, ROWS + 16, HD), BF16),
            pltpu.VMEM((ROWS + 16, HD), BF16),
            pltpu.VMEM((16, 16, HD), BF16),
            pltpu.VMEM((16, 16, HD), BF16),
            pltpu.VMEM((32, 16, HD), BF16),
            pltpu.SemaphoreType.DMA((5,)),
            pltpu.SemaphoreType.DMA,
            pltpu.SemaphoreType.DMA((8,)),
            pltpu.SemaphoreType.DMA,
            pltpu.SemaphoreType.DMA((len(PARTS),)),
            pltpu.SemaphoreType.DMA,
            pltpu.SemaphoreType.DMA,
            pltpu.SemaphoreType.DMA((2,)),
        ],
        compiler_params=pltpu.CompilerParams(
            collective_id=0, has_side_effects=True, vmem_limit_bytes=56541184
        ),
    )(rows, kv_cache[0], context_length, block_count, anchor_codes, delta_codes, block_scale)
    return out.reshape(4, STEPS, HD).swapaxes(0, 1).reshape(STEPS, 1, 4 * HD)


def solution(mesh):
    placed = (
        P(None, "req", None),
        P("req", "seq", None),
        P("req"),
        P("req"),
        P(None, "req", "seq"),
        P(None, "req", None, "seq"),
        P(None, "req", "seq"),
    )
    return jax.shard_map(
        shards, mesh=mesh, in_specs=placed, out_specs=P(None, "req", "seq"), check_vma=False
    )
```
